32 devices in a mesh: parts: 2 (over y), freq: 4 (over x, core), sx: 4 (over z).
Axes of the slice: x: 2, y: 2, z: 4, core: 2. Of those that a mesh axis runs over, the one named last changes fastest.
Arguments:
- design_density: float32 [64, 8, 1024], P(None, 'sx', 'parts'), parts along dimension 2, may hold values from 0.3 to 1
- observation: float32 [64, 8, 1024], P(None, 'sx', 'parts'), parts along dimension 2, may hold values from 0.1 to 1
- source: float32 [64, 8, 1024], P(None, 'sx', 'parts'), parts along dimension 2, may hold values from -6 to 6
- amplitude: float32 [8, 2], P('freq'), may hold values from -1 to 1
- omega_sq: float32 [8], P('freq'), may hold values from 0.5 to 2
- coupling: float32 [7, 64, 64], replicated, may hold values from -0.25 to 0.25
- inverse_blocks: float32 [8, 2, 64, 64], P('freq'), may hold values from -0.375 to 0.375
- primal_field: float32 [8, 2, 64, 8, 1024], P('freq', None, None, 'sx', 'parts'), parts along dimension 4, may hold values from -6 to 6
- adjoint_field: float32 [8, 2, 64, 8, 1024], P('freq', None, None, 'sx', 'parts'), parts along dimension 4, may hold values from -6 to 6
Outputs:
- density_gradient: float32 [64, 8, 1024], P('freq', 'sx', 'parts'), parts along dimension 2
The draws below stay inside these ranges and needn't reach their ends.
There are 2 independent parts, one for each index of `parts`. The reference program is written for one: setup_inputs(seed, part) draws one part's arguments, and reference() takes and returns one part's arrays. A program takes and returns all parts, laid end to end along the dimension named above; an argument that names none is the same for every part. Nothing has to cross between parts.
All inputs are finite; a program needn't handle non-finite values.
Results may differ from the reference program's by a relative error of at most 0.0001.
Values sent between devices are 32-bit elements; how exact they have to be, the bound alone decides.
A program may use at most 64 MiB of HBM per device.

```python
import math
import jax
import jax.numpy as jnp
from jax import lax

NODES = 64
COUPLED = 7
BZ = 32
FREQS = 8
NXB = 8
NYZ = 512


def block_levels(rng, shape, split, least, top_value):
    def one(dim, parts):
        steps = jax.random.uniform(jax.random.fold_in(jax.random.fold_in(rng, 6), dim), (parts,), jnp.float32, least / len(split), top_value / len(split))
        return jnp.repeat(jnp.exp(steps), shape[dim] // parts).reshape((-1,) + (1,) * (len(shape) - dim - 1))

    factor_of = one(*split[0])
    for cut in split[1:]:
        factor_of = factor_of * one(*cut)
    return factor_of


def scatter_about(own_key, dims, width, most, cuts=(), kind=jnp.bfloat16):
    array = width * jax.random.normal(own_key, dims, jnp.float32)
    if cuts:
        array = array * block_levels(own_key, dims, cuts, -0.22, 0.18)
    return jnp.clip(array, -most, most).astype(kind)


def setup_inputs(seed: int = 0, part: int = 0) -> dict:
    seeds = jax.random.split(jax.random.key(seed), 10)
    part_keys = jax.random.split(jax.random.fold_in(seeds[9], part), 10)
    return {
        "design_density": jnp.clip(0.3 + 0.7 * jax.random.uniform(part_keys[0], (NODES, NXB, NYZ), jnp.float32) ** block_levels(part_keys[0], (NODES, NXB, NYZ), ((1, 4),), -0.2, 0.2), 0.3, 1.0),
        "observation": jnp.clip(0.1 + 0.9 * jax.random.uniform(part_keys[1], (NODES, NXB, NYZ), jnp.float32) ** block_levels(part_keys[1], (NODES, NXB, NYZ), ((1, 4),), -0.2, 0.2), 0.1, 1.0),
        "source": scatter_about(part_keys[2], (NODES, NXB, NYZ), 1.0, 6.0, ((1, 4),), jnp.float32),
        "amplitude": jnp.clip(jax.random.uniform(seeds[3], (FREQS, 2), jnp.float32, -1.0, 1.0) * block_levels(seeds[3], (FREQS, 2), ((0, 4),), -0.4, 0.0), -1.0, 1.0),
        "omega_sq": jnp.clip(jnp.exp(math.log(2.0) - 1.3862944 * jax.random.uniform(seeds[4], (FREQS,), jnp.float32) ** block_levels(seeds[4], (FREQS,), ((0, 4),), -0.2, 0.2)), 0.5, 2.0),
        "coupling": scatter_about(seeds[5], (COUPLED, NODES, NODES), (COUPLED * NODES) ** -0.5, 0.25, (), jnp.float32),
        "inverse_blocks": scatter_about(seeds[6], (FREQS, 2, NODES, NODES), (4 * NODES) ** -0.5, 0.375, ((0, 4),), jnp.float32),
        "primal_field": scatter_about(part_keys[7], (FREQS, 2, NODES, NXB, NYZ), 1.0, 6.0, ((0, 4), (3, 4)), jnp.float32),
        "adjoint_field": scatter_about(part_keys[8], (FREQS, 2, NODES, NXB, NYZ), 1.0, 6.0, ((0, 4), (3, 4)), jnp.float32),
    }


BETA = 0.5


def shifted(values, offset, depth_blocks):
    length = values.shape[-1]
    padding = [(0, 0)] * (values.ndim - 1)
    if offset > 0:
        result = jnp.pad(values[..., offset:], padding + [(0, offset)])
    else:
        result = jnp.pad(values[..., :offset], padding + [(-offset, 0)])
    if abs(offset) == 1:
        column = jnp.arange(length) % depth_blocks + offset
        result = jnp.where((column >= 0) & (column < depth_blocks), result, jnp.zeros_like(result))
    return result


def neighbour_piece(extended, middle, direction, depth_blocks, transpose):
    orientation = -1 if transpose else 1
    if direction == 0:
        return middle
    if direction == 1:
        return extended[..., 2:, :] if transpose else extended[..., :-2, :]
    if direction == 2:
        return extended[..., :-2, :] if transpose else extended[..., 2:, :]
    offsets = [0, 0, 0, -depth_blocks, depth_blocks, -1, 1]
    return shifted(middle, orientation * offsets[direction], depth_blocks)


def stiffness_sum(coupling, extended, depth_blocks, transpose):
    middle = extended[..., 1:-1, :]
    pattern = "qp,fcqxy->fcpxy" if transpose else "pq,fcqxy->fcpxy"
    summed = jnp.zeros(middle.shape, middle.dtype)
    for direction in range(coupling.shape[0]):
        piece = neighbour_piece(extended, middle, direction, depth_blocks, transpose)
        summed = summed + jnp.einsum(pattern, coupling[direction], piece, precision=lax.Precision.HIGHEST)
    return summed


def mass_term(density, omega_sq, fields):
    realpart = fields[:, 0] + BETA * fields[:, 1]
    imagpart = fields[:, 1] - BETA * fields[:, 0]
    weights = omega_sq[:, None, None, None] * density[None]
    return jnp.stack([weights * realpart, weights * imagpart], axis=1)


def precondition(inverse_blocks, residual, transpose):
    pattern = "fqp,fqxy->fpxy" if transpose else "fpq,fqxy->fpxy"

    def product(matrix, values):
        return jnp.einsum(pattern, matrix, values, precision=lax.Precision.HIGHEST)

    inverse_real = inverse_blocks[:, 0]
    inverse_imag = inverse_blocks[:, 1]
    out_real = product(inverse_real, residual[:, 0]) - product(inverse_imag, residual[:, 1])
    out_imag = product(inverse_real, residual[:, 1]) + product(inverse_imag, residual[:, 0])
    return jnp.stack([out_real, out_imag], axis=1)


def gradient_terms(density, omega_sq, primal, adjoint, weighted):
    stiffness_part = 3.0 * density * density * (primal[:, 0] * weighted[:, 0] - primal[:, 1] * weighted[:, 1])
    bilinear = adjoint[:, 0] * primal[:, 0] - adjoint[:, 1] * primal[:, 1]
    crossed = adjoint[:, 0] * primal[:, 1] + adjoint[:, 1] * primal[:, 0]
    mass_part = omega_sq[:, None, None, None] * (bilinear + BETA * crossed)
    return jnp.sum(stiffness_part - mass_part, axis=0)


def reference(design_density, observation, source, amplitude, omega_sq, coupling, inverse_blocks, primal_field, adjoint_field):
    stiffen = design_density ** 3
    plane_pad = [(0, 0), (0, 0), (0, 0), (1, 1), (0, 0)]
    extended = jnp.pad(stiffen * primal_field, plane_pad)
    applied = stiffness_sum(coupling, extended, BZ, False) - mass_term(design_density, omega_sq, primal_field)
    forcing = amplitude[:, :, None, None, None] * source
    primal_new = primal_field + precondition(inverse_blocks, forcing - applied, False)
    adjoint_load = -observation * primal_new
    applied_adj = stiffen * stiffness_sum(coupling, jnp.pad(adjoint_field, plane_pad), BZ, True) - mass_term(design_density, omega_sq, adjoint_field)
    adjoint_new = adjoint_field + precondition(inverse_blocks, adjoint_load - applied_adj, True)
    weighted = stiffness_sum(coupling, jnp.pad(adjoint_new, plane_pad), BZ, True)
    return gradient_terms(design_density, omega_sq, primal_new, adjoint_new, weighted)
```

```python
import functools

import jax
import jax.numpy as jnp
from jax import lax
from jax.experimental import pallas as pl
from jax.experimental.pallas import tpu as pltpu
from jax.sharding import PartitionSpec as P

BZ = 32
BETA = 0.5
MESH = pl.DeviceIdType.MESH
PIECES = 2


def split(v):
    hi = v.astype(jnp.bfloat16)
    lo = (v - hi.astype(jnp.float32)).astype(jnp.bfloat16)
    return hi, lo


def left_operand(m):
    hi, lo = split(m)
    return jnp.concatenate(
        [jnp.concatenate([hi, hi], axis=1), jnp.concatenate([lo, jnp.zeros_like(lo)], axis=1)], axis=0
    )


def folded_dot(left, right):
    r = jnp.dot(left, right, preferred_element_type=jnp.float32)
    half = r.shape[0] // 2
    return r[:half] + r[half:]


def kernel(
    nf, nsx,
    amp, om, den_h, obs_h, src_h, cpl, inv, p_h, a_h,
    out_h,
    den, obs, src, p, a, sp, pn, an, rp, ra, hal, lk, lh, lp, grad, got, osum,
    small_sem, field_sem, send_h, recv_h, send_g, recv_g, out_sem,
):
    F, X, _, Q, N = p.shape
    rows = Q // nf
    me_f, me_s = lax.axis_index("freq"), lax.axis_index("sx")
    has = (me_s > 0, me_s < nsx - 1)

    smalls = []
    for i, (h, v) in enumerate(((den_h, den), (obs_h, obs), (src_h, src))):
        smalls.append([pltpu.make_async_copy(h.at[:, x, :], v.at[x], small_sem.at[i, x]) for x in range(X)])
    fields = [
        [[pltpu.make_async_copy(h.at[f, :, :, x, :], v.at[f, x], field_sem.at[i, f, x]) for x in range(X)] for f in range(F)]
        for i, (h, v) in enumerate(((p_h, p), (a_h, a)))
    ]

    def start(copies):
        for c in copies:
            c.start()

    def wait(copies):
        for c in copies:
            c.wait()

    start(fields[1][0])
    start(smalls[0])
    start(fields[0][0])
    start(fields[1][1])
    start(fields[0][1])
    start(smalls[2])
    start(smalls[1])

    barrier = pltpu.get_barrier_semaphore()
    for k in range(1, nf):
        pl.semaphore_signal(barrier, inc=1, device_id={"freq": lax.rem(me_f + k, nf)}, device_id_type=MESH)

    @pl.when(has[0])
    def _():
        pl.semaphore_signal(barrier, inc=1, device_id={"sx": me_s - 1}, device_id_type=MESH)

    @pl.when(has[1])
    def _():
        pl.semaphore_signal(barrier, inc=1, device_id={"sx": me_s + 1}, device_id_type=MESH)

    pl.semaphore_wait(barrier, nf - 1 + has[0].astype(jnp.int32) + has[1].astype(jnp.int32))

    def halo_copy(kind, f, side, piece=None):
        v = (a, sp, an)[kind]
        x, to = (X - 1, me_s + 1) if side == 0 else (0, me_s - 1)
        s, d = v.at[f, x], hal.at[kind, f, side]
        if piece is not None:
            cols = pl.ds(piece * (N // PIECES), N // PIECES)
            s, d = s.at[:, :, cols], d.at[:, :, cols]
        n = piece or 0
        return pltpu.make_async_remote_copy(
            src_ref=s, dst_ref=d, send_sem=send_h.at[kind, f, side, n], recv_sem=recv_h.at[kind, f, side, n],
            device_id={"sx": to}, device_id_type=MESH,
        )

    def halo(kind, f, do, piece=None):
        for side in range(2):
            there = has[side] if do == "wait_recv" else has[1 - side]

            @pl.when(there)
            def _():
                getattr(halo_copy(kind, f, side, piece), do)()

    def stiff(x):
        d = den[x]
        return d * d * d

    for f in range(F):
        wait(fields[1][f])
        halo(0, f, "start")
        if f == 0:
            wait(smalls[0])
        wait(fields[0][f])
        for x in range(X):
            s = stiff(x)
            for c in range(2):
                sp[f, x, c] = s * p[f, x, c]
        halo(1, f, "start")

    for side in range(2):

        @pl.when(jnp.logical_not(has[side]))
        def _():
            for kind in range(3):
                for f in range(F):
                    hal[kind, f, side] = jnp.zeros((2, Q, N), jnp.float32)

    cs = [cpl[d] for d in range(7)]
    ct = [c.T for c in cs]
    for j, order in enumerate((
        (cs[0], cs[3], cs[4], cs[5], cs[6], (cs[2], cs[1])),
        (ct[0], ct[4], ct[3], ct[6], ct[5], (ct[1], ct[2])),
    )):
        common = [left_operand(m) for m in order[:5]]
        other = [left_operand(m) for m in order[5]]
        for x in range(X):
            lk[j, x] = jnp.concatenate(common + [other[x]], axis=1)
            lh[j, x] = other[1 - x]
    for f in range(F):
        re, im = inv[f, 0], inv[f, 1]
        for j, (r, i) in enumerate(((re, im), (re.T, im.T))):
            lp[j, f] = left_operand(
                jnp.concatenate([jnp.concatenate([r, -i], axis=1), jnp.concatenate([i, r], axis=1)], axis=0)
            )

    column = lax.broadcasted_iota(jnp.int32, (Q, N), 1)
    place = column % BZ

    def local_sum(j, v, f, x, c):
        own, other = v[f, x, c], v[f, 1 - x, c]
        parts = [
            own,
            jnp.where(column >= BZ, pltpu.roll(own, BZ, 1), 0.0),
            jnp.where(column < N - BZ, pltpu.roll(own, N - BZ, 1), 0.0),
            jnp.where(place != 0, pltpu.roll(own, 1, 1), 0.0),
            jnp.where(place != BZ - 1, pltpu.roll(own, N - 1, 1), 0.0),
            other,
        ]
        right = jnp.concatenate([h for m in parts for h in split(m)], axis=0)
        return folded_dot(lk[j, x], right)

    def halo_sum(j, values, x):
        return folded_dot(lh[j, x], jnp.concatenate(split(values), axis=0))

    def mass(w, re, im):
        return w * (re + BETA * im), w * (im - BETA * re)

    wait(smalls[2])

    def residuals(i, carry):
        f, x = i // X, i % X
        d = den[x]
        w = om[f] * d
        mp = mass(w, p[f, x, 0], p[f, x, 1])
        ma = mass(w, a[f, x, 0], a[f, x, 1])
        s = d * d * d
        for c in range(2):
            rp[f, x, c] = amp[f, c] * src[x] - local_sum(0, sp, f, x, c) + mp[c]
            ra[f, x, c] = ma[c] - s * local_sum(1, a, f, x, c)
        return carry

    lax.fori_loop(0, F * X, residuals, 0)
    wait(smalls[1])

    for f in range(F):
        halo(0, f, "wait_recv")
        halo(1, f, "wait_recv")

        def sweep(x, carry, f=f):
            r = [rp[f, x, c] - halo_sum(0, hal[1, f, x, c], x) for c in range(2)]
            step = folded_dot(lp[0, f], jnp.concatenate(split(jnp.concatenate(r, axis=0)), axis=0))
            new = [p[f, x, c] + step[c * Q:(c + 1) * Q] for c in range(2)]
            s, o = stiff(x), obs[x]
            r = [ra[f, x, c] - s * halo_sum(1, hal[0, f, x, c], x) - o * new[c] for c in range(2)]
            step = folded_dot(lp[1, f], jnp.concatenate(split(jnp.concatenate(r, axis=0)), axis=0))
            for c in range(2):
                pn[f, x, c] = new[c]
                an[f, x, c] = a[f, x, c] + step[c * Q:(c + 1) * Q]
            return carry

        lax.fori_loop(0, X, sweep, 0)
        for piece in range(PIECES):
            halo(2, f, "start", piece)

    def gradient(x, carry):
        d = den[x]
        three = 3.0 * d * d
        total = jnp.zeros((Q, N), jnp.float32)
        for f in range(F):
            pr, pi, ar, ai = pn[f, x, 0], pn[f, x, 1], an[f, x, 0], an[f, x, 1]
            wr, wi = local_sum(1, an, f, x, 0), local_sum(1, an, f, x, 1)
            total = total + three * (pr * wr - pi * wi)
            total = total - om[f] * ((ar * pr - ai * pi) + BETA * (ar * pi + ai * pr))
        grad[x] = total
        return carry

    lax.fori_loop(0, X, gradient, 0)

    def share(k, piece):
        peer = lax.rem(me_f + k, nf)
        cols = pl.ds(piece * (N // PIECES), N // PIECES)
        return pltpu.make_async_remote_copy(
            src_ref=grad.at[:, pl.ds(pl.multiple_of(peer * rows, rows), rows), cols],
            dst_ref=got.at[k - 1, :, :, cols],
            send_sem=send_g.at[k - 1, piece], recv_sem=recv_g.at[k - 1, piece],
            device_id={"freq": peer}, device_id_type=MESH,
        )

    for f in range(F):
        for piece in range(PIECES):
            cols = slice(piece * (N // PIECES), (piece + 1) * (N // PIECES))
            halo(2, f, "wait_recv", piece)
            for x in range(X):
                d = den[x, :, cols]
                h = [halo_sum(1, hal[2, f, x, c, :, cols], x) for c in range(2)]
                grad[x, :, cols] += (3.0 * d * d) * (pn[f, x, 0, :, cols] * h[0] - pn[f, x, 1, :, cols] * h[1])
            if f == F - 1:
                for k in range(1, nf):
                    share(k, piece).start()

    mine = pl.ds(pl.multiple_of(me_f * rows, rows), rows)
    for piece in range(PIECES):
        cols = slice(piece * (N // PIECES), (piece + 1) * (N // PIECES))
        total = grad[:, mine, cols]
        for k in range(1, nf):
            share(k, piece).wait_recv()
            total = total + got[k - 1, :, :, cols]
        osum[:, :, cols] = total
    outs = [pltpu.make_async_copy(osum.at[x], out_h.at[:, x, :], out_sem.at[x]) for x in range(X)]
    start(outs)
    wait(outs)
    for f in range(F):
        halo(0, f, "wait_send")
        halo(1, f, "wait_send")
        for piece in range(PIECES):
            halo(2, f, "wait_send", piece)
    for piece in range(PIECES):
        for k in range(1, nf):
            share(k, piece).wait_send()


def shards(nf, nsx, den, obs, src, amp, om, cpl, inv, p, a):
    F, _, Q, X, N = p.shape
    rows = Q // nf
    f32, bf16, dma = jnp.float32, jnp.bfloat16, pltpu.SemaphoreType.DMA
    field = pltpu.VMEM((F, X, 2, Q, N), f32)
    plane = pltpu.VMEM((X, Q, N), f32)
    smem = pl.BlockSpec(memory_space=pltpu.SMEM)
    vmem = pl.BlockSpec(memory_space=pltpu.VMEM)
    anyw = pl.BlockSpec(memory_space=pl.ANY)
    columns = F * X * 2 * N
    return pl.pallas_call(
        functools.partial(kernel, nf, nsx),
        out_shape=jax.ShapeDtypeStruct((rows, X, N), f32),
        in_specs=[smem, smem, anyw, anyw, anyw, vmem, vmem, anyw, anyw],
        out_specs=anyw,
        scratch_shapes=[
            plane, plane, plane,
            field, field, field, field, field, field, field,
            pltpu.VMEM((3, F, 2, 2, Q, N), f32),
            pltpu.VMEM((2, X, 2 * Q, 12 * Q), bf16),
            pltpu.VMEM((2, X, 2 * Q, 2 * Q), bf16),
            pltpu.VMEM((2, F, 4 * Q, 4 * Q), bf16),
            plane,
            pltpu.VMEM((nf - 1, X, rows, N), f32),
            pltpu.VMEM((X, rows, N), f32),
            dma((3, X)), dma((2, F, X)),
            dma((3, F, 2, PIECES)), dma((3, F, 2, PIECES)),
            dma((nf - 1, PIECES)), dma((nf - 1, PIECES)),
            dma((X,)),
        ],
        compiler_params=pltpu.CompilerParams(
            collective_id=0, has_side_effects=True, vmem_limit_bytes=48 * 1024 * 1024
        ),
        cost_estimate=pl.CostEstimate(
            flops=2 * columns * (3 * 7 * Q * Q + 4 * Q * Q) * 3, bytes_accessed=4 * (2 * columns * Q), transcendentals=0
        ),
    )(amp, om, den, obs, src, cpl, inv, p, a)


def solution(mesh):
    in_specs = (
        P(None, "sx", "parts"),
        P(None, "sx", "parts"),
        P(None, "sx", "parts"),
        P("freq", None),
        P("freq"),
        P(),
        P("freq", None, None, None),
        P("freq", None, None, "sx", "parts"),
        P("freq", None, None, "sx", "parts"),
    )
    out_specs = P("freq", "sx", "parts")
    body = functools.partial(shards, mesh.shape["freq"], mesh.shape["sx"])
    return jax.shard_map(body, mesh=mesh, in_specs=in_specs, out_specs=out_specs, check_vma=False)
```

```python
import functools

import jax
import jax.numpy as jnp
from jax import lax
from jax.experimental import pallas as pl
from jax.experimental.pallas import tpu as pltpu
from jax.sharding import PartitionSpec as P

BZ = 32
BETA = 0.5
MESH = pl.DeviceIdType.MESH
PIECES = 2


def split(v):
    hi = v.astype(jnp.bfloat16)
    lo = (v - hi.astype(jnp.float32)).astype(jnp.bfloat16)
    return hi, lo


def left_operand(m):
    hi, lo = split(m)
    return jnp.concatenate(
        [jnp.concatenate([hi, hi], axis=1), jnp.concatenate([lo, jnp.zeros_like(lo)], axis=1)], axis=0
    )


def folded_dot(left, right):
    r = jnp.dot(left, right, preferred_element_type=jnp.float32)
    half = r.shape[0] // 2
    return r[:half] + r[half:]


def kernel(
    nf, nsx,
    amp_h, om_h, den_h, obs_h, src_h, cpl_h, inv_h, p_h, a_h,
    out_h,
    amp, om, cpl, inv,
    den, obs, src, p, a, sp, pn, an, rp, ra, hal, lk, lh, lp, grad, got, osum,
    param_sem, small_sem, field_sem, send_h, recv_h, send_g, recv_g, out_sem,
):
    F, X, _, Q, N = p.shape
    rows = Q // nf
    me_f, me_s = lax.axis_index("freq"), lax.axis_index("sx")
    has = (me_s > 0, me_s < nsx - 1)

    smalls = []
    for i, (h, v) in enumerate(((den_h, den), (obs_h, obs), (src_h, src))):
        smalls.append([pltpu.make_async_copy(h.at[:, x, :], v.at[x], small_sem.at[i, x]) for x in range(X)])
    fields = [
        [[pltpu.make_async_copy(h.at[f, :, :, x, :], v.at[f, x], field_sem.at[i, f, x]) for x in range(X)] for f in range(F)]
        for i, (h, v) in enumerate(((p_h, p), (a_h, a)))
    ]

    params = [
        pltpu.make_async_copy(h, v, param_sem.at[i])
        for i, (h, v) in enumerate(((amp_h, amp), (om_h, om), (cpl_h, cpl), (inv_h, inv)))
    ]

    def start(copies):
        for c in copies:
            c.start()

    def wait(copies):
        for c in copies:
            c.wait()

    start(fields[1][0])
    start(smalls[0])
    start(fields[0][0])
    start(fields[1][1])
    start(fields[0][1])
    start(params)
    start(smalls[2])
    start(smalls[1])

    barrier = pltpu.get_barrier_semaphore()
    for k in range(1, nf):
        pl.semaphore_signal(barrier, inc=1, device_id={"freq": lax.rem(me_f + k, nf)}, device_id_type=MESH)

    @pl.when(has[0])
    def _():
        pl.semaphore_signal(barrier, inc=1, device_id={"sx": me_s - 1}, device_id_type=MESH)

    @pl.when(has[1])
    def _():
        pl.semaphore_signal(barrier, inc=1, device_id={"sx": me_s + 1}, device_id_type=MESH)

    pl.semaphore_wait(barrier, nf - 1 + has[0].astype(jnp.int32) + has[1].astype(jnp.int32))

    def halo_copy(kind, f, side, piece=None):
        v = (a, sp, an)[kind]
        x, to = (X - 1, me_s + 1) if side == 0 else (0, me_s - 1)
        s, d = v.at[f, x], hal.at[kind, f, side]
        if piece is not None:
            cols = pl.ds(piece * (N // PIECES), N // PIECES)
            s, d = s.at[:, :, cols], d.at[:, :, cols]
        n = piece or 0
        return pltpu.make_async_remote_copy(
            src_ref=s, dst_ref=d, send_sem=send_h.at[kind, f, side, n], recv_sem=recv_h.at[kind, f, side, n],
            device_id={"sx": to}, device_id_type=MESH,
        )

    def halo(kind, f, do, piece=None):
        for side in range(2):
            there = has[side] if do == "wait_recv" else has[1 - side]

            @pl.when(there)
            def _():
                getattr(halo_copy(kind, f, side, piece), do)()

    def stiff(x):
        d = den[x]
        return d * d * d

    def stiffened(f):
        wait(fields[0][f])
        for x in range(X):
            s = stiff(x)
            for c in range(2):
                sp[f, x, c] = s * p[f, x, c]

    wait(fields[1][0])
    halo(0, 0, "start")
    wait(smalls[0])
    stiffened(0)
    halo(1, 0, "start")
    for f in range(1, F):
        wait(fields[1][f])
        stiffened(f)

    for side in range(2):

        @pl.when(jnp.logical_not(has[side]))
        def _():
            for kind in range(3):
                for f in range(F):
                    hal[kind, f, side] = jnp.zeros((2, Q, N), jnp.float32)

    wait(params)

    cs = [cpl[d] for d in range(7)]
    ct = [c.T for c in cs]
    for j, order in enumerate((
        (cs[0], cs[3], cs[4], cs[5], cs[6], (cs[2], cs[1])),
        (ct[0], ct[4], ct[3], ct[6], ct[5], (ct[1], ct[2])),
    )):
        common = [left_operand(m) for m in order[:5]]
        other = [left_operand(m) for m in order[5]]
        for x in range(X):
            lk[j, x] = jnp.concatenate(common + [other[x]], axis=1)
            lh[j, x] = other[1 - x]
    for f in range(F):
        re, im = inv[f, 0], inv[f, 1]
        for j, (r, i) in enumerate(((re, im), (re.T, im.T))):
            lp[j, f] = left_operand(
                jnp.concatenate([jnp.concatenate([r, -i], axis=1), jnp.concatenate([i, r], axis=1)], axis=0)
            )

    column = lax.broadcasted_iota(jnp.int32, (Q, N), 1)
    place = column % BZ

    def local_sum(j, v, f, x, c):
        own, other = v[f, x, c], v[f, 1 - x, c]
        parts = [
            own,
            jnp.where(column >= BZ, pltpu.roll(own, BZ, 1), 0.0),
            jnp.where(column < N - BZ, pltpu.roll(own, N - BZ, 1), 0.0),
            jnp.where(place != 0, pltpu.roll(own, 1, 1), 0.0),
            jnp.where(place != BZ - 1, pltpu.roll(own, N - 1, 1), 0.0),
            other,
        ]
        right = jnp.concatenate([h for m in parts for h in split(m)], axis=0)
        return folded_dot(lk[j, x], right)

    def halo_sum(j, values, x):
        return folded_dot(lh[j, x], jnp.concatenate(split(values), axis=0))

    def mass(w, re, im):
        return w * (re + BETA * im), w * (im - BETA * re)

    def residuals(x, carry, f):
        d = den[x]
        w = om[f] * d
        mp = mass(w, p[f, x, 0], p[f, x, 1])
        ma = mass(w, a[f, x, 0], a[f, x, 1])
        s = d * d * d
        for c in range(2):
            rp[f, x, c] = amp[f, c] * src[x] - local_sum(0, sp, f, x, c) + mp[c]
            ra[f, x, c] = ma[c] - s * local_sum(1, a, f, x, c)
        return carry

    def sweep(x, carry, f):
        r = [rp[f, x, c] - halo_sum(0, hal[1, f, x, c], x) for c in range(2)]
        step = folded_dot(lp[0, f], jnp.concatenate(split(jnp.concatenate(r, axis=0)), axis=0))
        new = [p[f, x, c] + step[c * Q:(c + 1) * Q] for c in range(2)]
        s, o = stiff(x), obs[x]
        r = [ra[f, x, c] - s * halo_sum(1, hal[0, f, x, c], x) - o * new[c] for c in range(2)]
        step = folded_dot(lp[1, f], jnp.concatenate(split(jnp.concatenate(r, axis=0)), axis=0))
        for c in range(2):
            pn[f, x, c] = new[c]
            an[f, x, c] = a[f, x, c] + step[c * Q:(c + 1) * Q]
        return carry

    def gradient(x, carry, f):
        d = den[x]
        pr, pi, ar, ai = pn[f, x, 0], pn[f, x, 1], an[f, x, 0], an[f, x, 1]
        wr, wi = local_sum(1, an, f, x, 0), local_sum(1, an, f, x, 1)
        total = (3.0 * d * d) * (pr * wr - pi * wi)
        total = total - om[f] * ((ar * pr - ai * pi) + BETA * (ar * pi + ai * pr))
        grad[x] = total if f == 0 else grad[x] + total
        return carry

    def planes(body, f):
        lax.fori_loop(0, X, functools.partial(body, f=f), 0)

    wait(smalls[2])
    planes(residuals, 0)
    for f in range(1, F):
        halo(0, f - 1, "wait_send")
        halo(0, f, "start")
        planes(residuals, f)
        halo(1, f - 1, "wait_send")
        halo(1, f, "start")
    wait(smalls[1])
    for f in range(F):
        halo(0, f, "wait_recv")
        halo(1, f, "wait_recv")
        planes(sweep, f)
        if f == F - 2:
            planes(gradient, f)
            halo(0, F - 1, "wait_send")
            halo(1, F - 1, "wait_send")
        for piece in range(PIECES):
            halo(2, f, "start", piece)
        if f != F - 2:
            planes(gradient, f)

    def share(k, piece):
        peer = lax.rem(me_f + k, nf)
        cols = pl.ds(piece * (N // PIECES), N // PIECES)
        return pltpu.make_async_remote_copy(
            src_ref=grad.at[:, pl.ds(pl.multiple_of(peer * rows, rows), rows), cols],
            dst_ref=got.at[k - 1, :, :, cols],
            send_sem=send_g.at[k - 1, piece], recv_sem=recv_g.at[k - 1, piece],
            device_id={"freq": peer}, device_id_type=MESH,
        )

    for f in range(F):
        for piece in range(PIECES):
            cols = slice(piece * (N // PIECES), (piece + 1) * (N // PIECES))
            halo(2, f, "wait_recv", piece)
            for x in range(X):
                d = den[x, :, cols]
                h = [halo_sum(1, hal[2, f, x, c, :, cols], x) for c in range(2)]
                grad[x, :, cols] += (3.0 * d * d) * (pn[f, x, 0, :, cols] * h[0] - pn[f, x, 1, :, cols] * h[1])
            if f == F - 1:
                for k in range(1, nf):
                    share(k, piece).start()

    mine = pl.ds(pl.multiple_of(me_f * rows, rows), rows)
    for piece in range(PIECES):
        cols = slice(piece * (N // PIECES), (piece + 1) * (N // PIECES))
        total = grad[:, mine, cols]
        for k in range(1, nf):
            share(k, piece).wait_recv()
            total = total + got[k - 1, :, :, cols]
        osum[:, :, cols] = total
    outs = [pltpu.make_async_copy(osum.at[x], out_h.at[:, x, :], out_sem.at[x]) for x in range(X)]
    start(outs)
    wait(outs)
    for f in range(F):
        for piece in range(PIECES):
            halo(2, f, "wait_send", piece)
    for piece in range(PIECES):
        for k in range(1, nf):
            share(k, piece).wait_send()


def shards(nf, nsx, den, obs, src, amp, om, cpl, inv, p, a):
    F, _, Q, X, N = p.shape
    rows = Q // nf
    f32, bf16, dma = jnp.float32, jnp.bfloat16, pltpu.SemaphoreType.DMA
    field = pltpu.VMEM((F, X, 2, Q, N), f32)
    plane = pltpu.VMEM((X, Q, N), f32)
    hbm = pl.BlockSpec(memory_space=pltpu.HBM)
    columns = F * X * 2 * N
    return pl.pallas_call(
        functools.partial(kernel, nf, nsx),
        out_shape=jax.ShapeDtypeStruct((rows, X, N), f32),
        in_specs=[hbm] * 9,
        out_specs=hbm,
        scratch_shapes=[
            pltpu.SMEM(amp.shape, f32), pltpu.SMEM(om.shape, f32), pltpu.VMEM(cpl.shape, f32), pltpu.VMEM(inv.shape, f32),
            plane, plane, plane,
            field, field, field, field, field, field, field,
            pltpu.VMEM((3, F, 2, 2, Q, N), f32),
            pltpu.VMEM((2, X, 2 * Q, 12 * Q), bf16),
            pltpu.VMEM((2, X, 2 * Q, 2 * Q), bf16),
            pltpu.VMEM((2, F, 4 * Q, 4 * Q), bf16),
            plane,
            pltpu.VMEM((nf - 1, X, rows, N), f32),
            pltpu.VMEM((X, rows, N), f32),
            dma((4,)), dma((3, X)), dma((2, F, X)),
            dma((3, F, 2, PIECES)), dma((3, F, 2, PIECES)),
            dma((nf - 1, PIECES)), dma((nf - 1, PIECES)),
            dma((X,)),
        ],
        compiler_params=pltpu.CompilerParams(
            collective_id=0, has_side_effects=True, vmem_limit_bytes=60 * 1024 * 1024
        ),
        cost_estimate=pl.CostEstimate(
            flops=2 * columns * (3 * 7 * Q * Q + 4 * Q * Q) * 3, bytes_accessed=4 * (2 * columns * Q), transcendentals=0
        ),
    )(amp, om, den, obs, src, cpl, inv, p, a)


def solution(mesh):
    in_specs = (
        P(None, "sx", "parts"),
        P(None, "sx", "parts"),
        P(None, "sx", "parts"),
        P("freq", None),
        P("freq"),
        P(),
        P("freq", None, None, None),
        P("freq", None, None, "sx", "parts"),
        P("freq", None, None, "sx", "parts"),
    )
    out_specs = P("freq", "sx", "parts")
    body = functools.partial(shards, mesh.shape["freq"], mesh.shape["sx"])
    return jax.shard_map(body, mesh=mesh, in_specs=in_specs, out_specs=out_specs, check_vma=False)
```

```python
import functools

import jax
import jax.numpy as jnp
from jax import lax
from jax.experimental import pallas as pl
from jax.experimental.pallas import tpu as pltpu
from jax.sharding import PartitionSpec as P

BZ = 32
BETA = 0.5
MESH = pl.DeviceIdType.MESH
PIECES = 2


def split(v):
    hi = v.astype(jnp.bfloat16)
    lo = (v - hi.astype(jnp.float32)).astype(jnp.bfloat16)
    return hi, lo


def left_operand(m):
    hi, lo = split(m)
    return jnp.concatenate(
        [jnp.concatenate([hi, hi], axis=1), jnp.concatenate([lo, jnp.zeros_like(lo)], axis=1)], axis=0
    )


def folded_dot(left, right):
    r = jnp.dot(left, right, preferred_element_type=jnp.float32)
    half = r.shape[0] // 2
    return r[:half] + r[half:]


def kernel(
    nf, nsx,
    amp_h, om_h, den_h, obs_h, src_h, cpl_h, inv_h, p_h, a_h,
    got,
    amp, om, cpl, inv,
    den, obs, src, p, a, sp, pn, an, rp, ra, hal, lk, lh, lp, grad,
    param_sem, small_sem, field_sem, send_h, recv_h, send_g, recv_g, out_sem,
):
    F, X, _, Q, N = p.shape
    rows = Q // nf
    me_f, me_s = lax.axis_index("freq"), lax.axis_index("sx")
    has = (me_s > 0, me_s < nsx - 1)

    smalls = []
    for i, (h, v) in enumerate(((den_h, den), (obs_h, obs), (src_h, src))):
        smalls.append([pltpu.make_async_copy(h.at[:, x, :], v.at[x], small_sem.at[i, x]) for x in range(X)])
    fields = [
        [[pltpu.make_async_copy(h.at[f, :, :, x, :], v.at[f, x], field_sem.at[i, f, x]) for x in range(X)] for f in range(F)]
        for i, (h, v) in enumerate(((p_h, p), (a_h, a)))
    ]

    params = [
        pltpu.make_async_copy(h, v, param_sem.at[i])
        for i, (h, v) in enumerate(((amp_h, amp), (om_h, om), (cpl_h, cpl), (inv_h, inv)))
    ]

    def start(copies):
        for c in copies:
            c.start()

    def wait(copies):
        for c in copies:
            c.wait()

    start(fields[1][0])
    start(smalls[0])
    start(fields[0][0])
    start(fields[1][1])
    start(fields[0][1])
    start(params)
    start(smalls[2])
    start(smalls[1])

    barrier = pltpu.get_barrier_semaphore()
    for k in range(1, nf):
        pl.semaphore_signal(barrier, inc=1, device_id={"freq": lax.rem(me_f + k, nf)}, device_id_type=MESH)

    @pl.when(has[0])
    def _():
        pl.semaphore_signal(barrier, inc=1, device_id={"sx": me_s - 1}, device_id_type=MESH)

    @pl.when(has[1])
    def _():
        pl.semaphore_signal(barrier, inc=1, device_id={"sx": me_s + 1}, device_id_type=MESH)

    pl.semaphore_wait(barrier, nf - 1 + has[0].astype(jnp.int32) + has[1].astype(jnp.int32))

    def halo_copy(kind, f, side, piece=None):
        v = (a, sp, an)[kind]
        x, to = (X - 1, me_s + 1) if side == 0 else (0, me_s - 1)
        s, d = v.at[f, x], hal.at[kind, f, side]
        if piece is not None:
            cols = pl.ds(piece * (N // PIECES), N // PIECES)
            s, d = s.at[:, :, cols], d.at[:, :, cols]
        n = piece or 0
        return pltpu.make_async_remote_copy(
            src_ref=s, dst_ref=d, send_sem=send_h.at[kind, f, side, n], recv_sem=recv_h.at[kind, f, side, n],
            device_id={"sx": to}, device_id_type=MESH,
        )

    def halo(kind, f, do, piece=None):
        for side in range(2):
            there = has[side] if do == "wait_recv" else has[1 - side]

            @pl.when(there)
            def _():
                getattr(halo_copy(kind, f, side, piece), do)()

    def stiff(x):
        d = den[x]
        return d * d * d

    def stiffened(f):
        wait(fields[0][f])
        for x in range(X):
            s = stiff(x)
            for c in range(2):
                sp[f, x, c] = s * p[f, x, c]

    wait(fields[1][0])
    halo(0, 0, "start")
    wait(smalls[0])
    stiffened(0)
    halo(1, 0, "start")
    for f in range(1, F):
        wait(fields[1][f])
        stiffened(f)

    for side in range(2):

        @pl.when(jnp.logical_not(has[side]))
        def _():
            for kind in range(3):
                for f in range(F):
                    hal[kind, f, side] = jnp.zeros((2, Q, N), jnp.float32)

    wait(params)

    cs = [cpl[d] for d in range(7)]
    ct = [c.T for c in cs]
    for j, order in enumerate((
        (cs[0], cs[3], cs[4], cs[5], cs[6], (cs[2], cs[1])),
        (ct[0], ct[4], ct[3], ct[6], ct[5], (ct[1], ct[2])),
    )):
        common = [left_operand(m) for m in order[:5]]
        other = [left_operand(m) for m in order[5]]
        for x in range(X):
            lk[j, x] = jnp.concatenate(common + [other[x]], axis=1)
            lh[j, x] = other[1 - x]
    for f in range(F):
        re, im = inv[f, 0], inv[f, 1]
        for j, (r, i) in enumerate(((re, im), (re.T, im.T))):
            lp[j, f] = left_operand(
                jnp.concatenate([jnp.concatenate([r, -i], axis=1), jnp.concatenate([i, r], axis=1)], axis=0)
            )

    column = lax.broadcasted_iota(jnp.int32, (Q, N), 1)
    place = column % BZ

    def local_sum(j, v, f, x, c):
        own, other = v[f, x, c], v[f, 1 - x, c]
        parts = [
            own,
            jnp.where(column >= BZ, pltpu.roll(own, BZ, 1), 0.0),
            jnp.where(column < N - BZ, pltpu.roll(own, N - BZ, 1), 0.0),
            jnp.where(place != 0, pltpu.roll(own, 1, 1), 0.0),
            jnp.where(place != BZ - 1, pltpu.roll(own, N - 1, 1), 0.0),
            other,
        ]
        right = jnp.concatenate([h for m in parts for h in split(m)], axis=0)
        return folded_dot(lk[j, x], right)

    def halo_sum(j, values, x):
        return folded_dot(lh[j, x], jnp.concatenate(split(values), axis=0))

    def mass(w, re, im):
        return w * (re + BETA * im), w * (im - BETA * re)

    def residuals(x, carry, f):
        d = den[x]
        w = om[f] * d
        mp = mass(w, p[f, x, 0], p[f, x, 1])
        ma = mass(w, a[f, x, 0], a[f, x, 1])
        s = d * d * d
        for c in range(2):
            rp[f, x, c] = amp[f, c] * src[x] - local_sum(0, sp, f, x, c) + mp[c]
            ra[f, x, c] = ma[c] - s * local_sum(1, a, f, x, c)
        return carry

    def sweep(x, carry, f):
        r = [rp[f, x, c] - halo_sum(0, hal[1, f, x, c], x) for c in range(2)]
        step = folded_dot(lp[0, f], jnp.concatenate(split(jnp.concatenate(r, axis=0)), axis=0))
        new = [p[f, x, c] + step[c * Q:(c + 1) * Q] for c in range(2)]
        s, o = stiff(x), obs[x]
        r = [ra[f, x, c] - s * halo_sum(1, hal[0, f, x, c], x) - o * new[c] for c in range(2)]
        step = folded_dot(lp[1, f], jnp.concatenate(split(jnp.concatenate(r, axis=0)), axis=0))
        for c in range(2):
            pn[f, x, c] = new[c]
            an[f, x, c] = a[f, x, c] + step[c * Q:(c + 1) * Q]
        return carry

    def gradient(x, carry, f):
        d = den[x]
        pr, pi, ar, ai = pn[f, x, 0], pn[f, x, 1], an[f, x, 0], an[f, x, 1]
        wr, wi = local_sum(1, an, f, x, 0), local_sum(1, an, f, x, 1)
        total = (3.0 * d * d) * (pr * wr - pi * wi)
        total = total - om[f] * ((ar * pr - ai * pi) + BETA * (ar * pi + ai * pr))
        grad[x] = total if f == 0 else grad[x] + total
        return carry

    def pieces(f):
        return range(PIECES) if f == F - 1 else (None,)

    def planes(body, f):
        lax.fori_loop(0, X, functools.partial(body, f=f), 0)

    wait(smalls[2])
    planes(residuals, 0)
    for f in range(1, F):
        halo(0, f - 1, "wait_send")
        halo(0, f, "start")
        planes(residuals, f)
        halo(1, f - 1, "wait_send")
        halo(1, f, "start")
    wait(smalls[1])
    for f in range(F):
        halo(0, f, "wait_recv")
        halo(1, f, "wait_recv")
        planes(sweep, f)
        if f == F - 2:
            planes(gradient, f)
            halo(0, F - 1, "wait_send")
            halo(1, F - 1, "wait_send")
        for piece in pieces(f):
            halo(2, f, "start", piece)
        if f != F - 2:
            planes(gradient, f)

    def share(k, piece):
        peer = lax.rem(me_f + k, nf)
        cols = pl.ds(piece * (N // PIECES), N // PIECES)
        return pltpu.make_async_remote_copy(
            src_ref=grad.at[:, pl.ds(pl.multiple_of(peer * rows, rows), rows), cols],
            dst_ref=got.at[k - 1, :, :, cols],
            send_sem=send_g.at[k - 1, piece], recv_sem=recv_g.at[k - 1, piece],
            device_id={"freq": peer}, device_id_type=MESH,
        )

    for f in range(F):
        for piece in pieces(f):
            cols = slice(0, N) if piece is None else slice(piece * (N // PIECES), (piece + 1) * (N // PIECES))
            halo(2, f, "wait_recv", piece)
            for x in range(X):
                d = den[x, :, cols]
                h = [halo_sum(1, hal[2, f, x, c, :, cols], x) for c in range(2)]
                grad[x, :, cols] += (3.0 * d * d) * (pn[f, x, 0, :, cols] * h[0] - pn[f, x, 1, :, cols] * h[1])
            if f == F - 1:
                for k in range(1, nf):
                    share(k, piece).start()
    mine = pl.ds(pl.multiple_of(me_f * rows, rows), rows)
    own = pltpu.make_async_copy(grad.at[:, mine, :], got.at[nf - 1], out_sem)
    own.start()

    for piece in range(PIECES):
        for k in range(1, nf):
            share(k, piece).wait_recv()
    own.wait()
    for f in range(F):
        for piece in pieces(f):
            halo(2, f, "wait_send", piece)
    for piece in range(PIECES):
        for k in range(1, nf):
            share(k, piece).wait_send()


def shards(nf, nsx, den, obs, src, amp, om, cpl, inv, p, a):
    F, _, Q, X, N = p.shape
    rows = Q // nf
    f32, bf16, dma = jnp.float32, jnp.bfloat16, pltpu.SemaphoreType.DMA
    field = pltpu.VMEM((F, X, 2, Q, N), f32)
    plane = pltpu.VMEM((X, Q, N), f32)
    hbm = pl.BlockSpec(memory_space=pltpu.HBM)
    columns = F * X * 2 * N
    terms = pl.pallas_call(
        functools.partial(kernel, nf, nsx),
        out_shape=jax.ShapeDtypeStruct((nf, X, rows, N), f32),
        in_specs=[hbm] * 9,
        out_specs=hbm,
        scratch_shapes=[
            pltpu.SMEM(amp.shape, f32), pltpu.SMEM(om.shape, f32), pltpu.VMEM(cpl.shape, f32), pltpu.VMEM(inv.shape, f32),
            plane, plane, plane,
            field, field, field, field, field, field, field,
            pltpu.VMEM((3, F, 2, 2, Q, N), f32),
            pltpu.VMEM((2, X, 2 * Q, 12 * Q), bf16),
            pltpu.VMEM((2, X, 2 * Q, 2 * Q), bf16),
            pltpu.VMEM((2, F, 4 * Q, 4 * Q), bf16),
            plane,
            dma((4,)), dma((3, X)), dma((2, F, X)),
            dma((3, F, 2, PIECES)), dma((3, F, 2, PIECES)),
            dma((nf - 1, PIECES)), dma((nf - 1, PIECES)),
            dma,
        ],
        compiler_params=pltpu.CompilerParams(
            collective_id=0, has_side_effects=True, vmem_limit_bytes=60 * 1024 * 1024
        ),
        cost_estimate=pl.CostEstimate(
            flops=2 * columns * (3 * 7 * Q * Q + 4 * Q * Q) * 3, bytes_accessed=4 * (2 * columns * Q), transcendentals=0
        ),
    )(amp, om, den, obs, src, cpl, inv, p, a)
    return jnp.sum(terms, axis=0).transpose(1, 0, 2)


def solution(mesh):
    in_specs = (
        P(None, "sx", "parts"),
        P(None, "sx", "parts"),
        P(None, "sx", "parts"),
        P("freq", None),
        P("freq"),
        P(),
        P("freq", None, None, None),
        P("freq", None, None, "sx", "parts"),
        P("freq", None, None, "sx", "parts"),
    )
    out_specs = P("freq", "sx", "parts")
    body = functools.partial(shards, mesh.shape["freq"], mesh.shape["sx"])
    return jax.shard_map(body, mesh=mesh, in_specs=in_specs, out_specs=out_specs, check_vma=False)
```
